32 devices in a mesh: row: 8 (over z, y), col: 4 (over x, core).
Axes of the slice: x: 2, y: 2, z: 4, core: 2. Of those that a mesh axis runs over, the one named last changes fastest.
Arguments:
- anc_factor: float32 [8192, 4096], P('row', 'col'), may hold values from -0.09375 to 0.09375
- anc_solution: float32 [128, 12288], P('col', 'row'), may hold values from -6 to 6
- slot_row: int32 [8192], P('row'), may hold values from 0 to 1535, as said below
- tile_count: int32 [8], P('row'), may hold values from 2 to 8, as said below
- lower_factor: float32 [4, 1024, 4096], P(None, 'row', 'col'), may hold values from -0.109375 to 0.109375
- diag_inverse: float32 [4, 1024, 1024], P('col'), may hold values from -1.5 to 1.5, as said below
- rhs: float32 [128, 4096], P('row', 'col'), may hold values from -6 to 6
Outputs:
- solution: float32 [128, 4096], P('row', 'col')
The draws below stay inside these ranges and needn't reach their ends.
Inputs may be any that keep to these rules, and one draw needn't show every extreme that they name: `slot_row`: within each aligned block of 1024 entries the values are distinct, and some block holds 1535. `tile_count`: some entry equals 8 in every draw. Each block diag_inverse[t] is lower triangular with a positive diagonal.
All inputs are finite; a program needn't handle non-finite values.
Results may differ from the reference program's by a relative error of at most 0.0001.
Values sent between devices are 32-bit elements; how exact they have to be, the bound alone decides.
A program may use at most 64 MiB of HBM per device.

```python
import math
import jax
import jax.numpy as jnp
from jax import lax

PW = 1024
TILE = 128
TILES_DEV = 8
ANC_DEV = 1536
RHS = 128
SLOTS_DEV = 1024
PANELS = 4
NPIV = 4096
ANC_ROWS = 8192
PARENT_ROWS = 12288
N_ROW = 8


def draw_slot_row(key, part):
    count_rows = ANC_ROWS // SLOTS_DEV
    keys_all = jax.random.split(key, count_rows)

    def one_device(device_key):
        chosen = jax.random.permutation(device_key, ANC_DEV)[:SLOTS_DEV]
        present = jnp.any(chosen == ANC_DEV - 1)
        return jnp.where(present, chosen, chosen.at[SLOTS_DEV - 1].set(ANC_DEV - 1))
    return jax.vmap(one_device)(keys_all).reshape(-1).astype(jnp.int32)


def draw_tile_count(key, part):
    key_counts, key_pick = jax.random.split(jax.random.fold_in(key, 7))
    count_rows = ANC_ROWS // SLOTS_DEV
    counts = jax.random.randint(key_counts, (count_rows,), TILES_DEV // 4, TILES_DEV // 2 + 1)
    busiest = jax.random.randint(key_pick, (), 0, count_rows)
    return jnp.where(jnp.arange(count_rows) == busiest, TILES_DEV, counts).astype(jnp.int32)


def draw_diag_inverse(key, part):
    key_lower, key_diag = jax.random.split(jax.random.fold_in(key, 11))
    spread = jnp.clip(jax.random.normal(key_lower, (PANELS, PW, PW), jnp.float32), -2.5, 2.5)
    lower_part = jnp.tril(spread, -1) * (0.6 / math.sqrt(PW))
    diagonal = jax.random.uniform(key_diag, (PANELS, PW), jnp.float32, 0.6, 1.4)
    return lower_part + diagonal[:, :, None] * jnp.eye(PW, dtype=jnp.float32)[None, :, :]


def block_levels(own_key, extent, cuts, low, largest):
    factor_of, own = 1.0, jax.random.fold_in(own_key, 6)
    for dim, parts in cuts:
        heights = jnp.exp(jax.random.uniform(jax.random.fold_in(own, dim), (parts,), jnp.float32, low / len(cuts), largest / len(cuts)))
        factor_of = factor_of * jnp.repeat(heights, extent[dim] // parts).reshape([-1 if axis == dim else 1 for axis in range(len(extent))])
    return factor_of


def scatter_about(rng, extent, scale, limit, shards=(), kind=jnp.bfloat16):
    array = jax.random.normal(rng, extent, jnp.float32) * scale
    if len(shards) > 0:
        array = block_levels(rng, extent, shards, -0.22, 0.18) * array
    return jnp.clip(array, min=-limit, max=limit).astype(kind)


def setup_inputs(seed: int = 0) -> dict:
    key_list = jax.random.split(jax.random.key(seed), 8)
    anc_factor = scatter_about(key_list[0], (ANC_ROWS, NPIV), (ANC_ROWS // 2) ** -0.5, 0.09375, ((0, 8), (1, 4)), jnp.float32)
    anc_solution = scatter_about(key_list[1], (RHS, PARENT_ROWS), 1.0, 6.0, ((0, 4), (1, 8)), jnp.float32)
    slot_row = draw_slot_row(jax.random.fold_in(key_list[7], 71), 0)
    tile_count = draw_tile_count(jax.random.fold_in(key_list[7], 71), 0)
    lower_factor = scatter_about(key_list[4], (PANELS, PW, NPIV), (3 * PW) ** -0.5, 0.109375, ((1, 8), (2, 4)), jnp.float32)
    diag_inverse = draw_diag_inverse(jax.random.fold_in(key_list[7], 71), 0)
    rhs = scatter_about(key_list[6], (RHS, NPIV), 1.0, 6.0, ((0, 8), (1, 4)), jnp.float32)
    return dict(anc_factor=anc_factor, anc_solution=anc_solution, slot_row=slot_row, tile_count=tile_count, lower_factor=lower_factor, diag_inverse=diag_inverse, rhs=rhs)


def reference(anc_factor, anc_solution, slot_row, tile_count, lower_factor, diag_inverse, rhs):
    highest = lax.Precision.HIGHEST
    position = jnp.arange(N_ROW * SLOTS_DEV).astype(jnp.int32)
    owner_row = position // SLOTS_DEV
    parent_index = (owner_row * ANC_DEV + slot_row).astype(jnp.int32)
    alive_mask = ((position % SLOTS_DEV) < tile_count[owner_row] * TILE).astype(jnp.float32)
    selected = jnp.take(anc_solution, parent_index, axis=1) * alive_mask[None, :]
    updated = rhs - jnp.dot(selected, anc_factor, precision=highest, preferred_element_type=jnp.float32)
    solution = jnp.zeros((RHS, NPIV), jnp.float32)
    for target in range(PANELS - 1, -1, -1):
        offset = target * PW
        pending = updated[:, offset:offset + PW]
        if target < PANELS - 1:
            below_rows = lower_factor[target + 1:, :, offset:offset + PW].reshape(-1, PW)
            pending = pending - jnp.dot(solution[:, offset + PW:], below_rows, precision=highest, preferred_element_type=jnp.float32)
        solved = jnp.dot(pending, diag_inverse[target], precision=highest, preferred_element_type=jnp.float32)
        solution = solution.at[:, offset:offset + PW].set(solved)
    return solution
```

```python
import functools

import jax
import jax.numpy as jnp
from jax import lax
from jax.experimental import pallas as pl
from jax.experimental.pallas import tpu as pltpu
from jax.sharding import PartitionSpec as P

TILE = 128
LANES = 128
MESH = pl.DeviceIdType.MESH
F32 = jnp.float32
BF16 = jnp.bfloat16


def split(x):
    hi = x.astype(BF16)
    lo = (x - hi.astype(F32)).astype(BF16)
    return hi, lo


def mm(a, b):
    return jnp.dot(a, b, preferred_element_type=F32)


def kernel(
    group,
    n_row,
    n_col,
    slot_ref,
    count_ref,
    parent_ref,
    rhs_ref,
    anc_ref,
    low_ref,
    diag_ref,
    out_ref,
    anc_f,
    anc_h,
    anc_l,
    diag_f,
    diag_h,
    diag_l,
    low_all,
    low_s,
    fold_h,
    fold_l,
    par_s,
    sel,
    sel_s,
    part,
    part_in,
    pre_s,
    acc,
    red_in,
    solved,
    x_in,
    x_s,
    sem_anc,
    sem_diag,
    sem_low,
    sel_tx,
    sel_rx,
    low_tx,
    low_rx,
    part_tx,
    part_rx,
    red_tx,
    red_rx,
    x_tx,
    x_rx,
):
    row = lax.axis_index("row")
    col = lax.axis_index("col")
    n_z = n_row // group
    z = row // group
    y = row % group
    width = diag_f.shape[1]
    slots = sel.shape[2]
    share = rhs_ref.shape[0]
    n_rhs = share * n_row
    sub = share * n_z
    wide = min(256, width)
    steps = width // wide
    depth = x_in.shape[3]

    copy_anc = pltpu.make_async_copy(anc_ref, anc_f, sem_anc)
    copy_anc.start()
    copy_diag = pltpu.make_async_copy(diag_ref.at[0], diag_f, sem_diag)
    copy_diag.start()
    for k in range(1, n_col):
        pltpu.make_async_copy(low_ref.at[k], low_all.at[k, y], sem_low.at[k]).start()

    barrier = pltpu.get_barrier_semaphore()

    def greet(dev_row, dev_col):
        pl.semaphore_signal(barrier, inc=1, device_id=(dev_row, dev_col), device_id_type=MESH)

    for d in range(n_z):
        for e in range(n_col):
            if d or e:
                greet(lax.rem(z + d, n_z) * group + y, lax.rem(col + e, n_col))
    for d in range(1, group):
        greet(z * group + lax.rem(y + d, group), col)

    mine = sel.shape[1]
    hi, lo = split(parent_ref[...])
    par_s[0:mine, :] = hi
    par_s[mine:, :] = lo
    parents = parent_ref.shape[1]

    def select(n, carry):
        at = pl.ds(pl.multiple_of(n * wide, wide), wide)
        place = lax.broadcasted_iota(jnp.int32, (1, wide), 1) + n * wide
        wanted = jnp.where(place < count_ref[0] * TILE, slot_ref[:, at], -1)
        which = lax.broadcasted_iota(jnp.int32, (parents, wide), 0)
        hot = jnp.where(which == wanted, 1.0, 0.0).astype(BF16)
        both = mm(par_s[...], hot)
        sel[col, :, at] = both[0:mine] + both[mine:]
        return carry

    lax.fori_loop(0, slots // wide, select, 0)

    pl.semaphore_wait(barrier, n_z * n_col - 1 + group - 1)

    def sel_copy(owner, to):
        return pltpu.make_async_remote_copy(
            src_ref=sel.at[owner],
            dst_ref=sel.at[owner],
            send_sem=sel_tx.at[to],
            recv_sem=sel_rx.at[owner],
            device_id=(row, to),
            device_id_type=MESH,
        )

    def others_col(e):
        return lax.rem(col + e, n_col)

    for e in range(1, n_col):
        sel_copy(col, others_col(e)).start()

    def low_copy(k, owner, to):
        return pltpu.make_async_remote_copy(
            src_ref=low_ref.at[k],
            dst_ref=low_all.at[k, owner],
            send_sem=low_tx.at[k, to],
            recv_sem=low_rx.at[k, owner],
            device_id=(z * group + to, col),
            device_id_type=MESH,
        )

    for k in range(n_col - 1, 0, -1):

        @pl.when(col < k)
        def _():
            for d in range(1, group):
                low_copy(k, y, lax.rem(y + d, group)).start()

    def split_rows(src, dst_h, dst_l):
        rows = 128

        def body(i, carry):
            at = pl.ds(pl.multiple_of(i * rows, rows), rows)
            h, l = split(src[at, :])
            dst_h[at, :] = h
            dst_l[at, :] = l
            return carry

        lax.fori_loop(0, src.shape[0] // rows, body, 0)

    copy_anc.wait()
    split_rows(anc_f, anc_h, anc_l)

    for e in range(1, n_col):
        sel_copy(others_col(e), col).wait_recv()
    hi, lo = split(sel[...].reshape(n_rhs, slots))
    sel_s[0:n_rhs, :] = hi
    sel_s[n_rhs:, :] = lo
    for n in range(steps):
        at = slice(n * wide, (n + 1) * wide)
        both = mm(sel_s[...], anc_h[:, at])
        term = both[0:n_rhs] + both[n_rhs:] + mm(sel_s[0:n_rhs, :], anc_l[:, at])
        for r in range(n_row):
            part[r % group, r // group, :, at] = term[r * share : (r + 1) * share]

    def part_copy(owner, to):
        return pltpu.make_async_remote_copy(
            src_ref=part.at[to],
            dst_ref=part_in.at[owner],
            send_sem=part_tx.at[to],
            recv_sem=part_rx.at[owner],
            device_id=(z * group + to, col),
            device_id_type=MESH,
        )

    for d in range(1, group):
        part_copy(y, lax.rem(y + d, group)).start()

    copy_diag.wait()
    split_rows(diag_f, diag_h, diag_l)

    for d in range(1, group):
        part_copy(lax.rem(y + d, group), y).wait_recv()

    pre = part[y]
    for d in range(1, group):
        pre = pre + part_in[lax.rem(y + d, group)]
    zs = lax.broadcasted_iota(jnp.int32, (n_z, 1, 1), 0)
    pre = jnp.where(zs == z, rhs_ref[...][None], 0.0) - pre
    hi, lo = split(pre.reshape(sub, width))
    pre_s[0:sub, :] = hi
    pre_s[sub:, :] = lo
    for n in range(steps):
        at = slice(n * wide, (n + 1) * wide)
        below = slice(n * wide, width)
        both = mm(pre_s[:, below], diag_h[below, at])
        term = both[0:sub] + both[sub:] + mm(pre_s[0:sub, below], diag_l[below, at])
        acc[:, :, at] = term.reshape(n_z, share, wide)

    for k in range(1, n_col):
        pltpu.make_async_copy(low_ref.at[k], low_all.at[k, y], sem_low.at[k]).wait()

    def fold(i, carry):
        k = n_col - 1 - i
        for d in range(1, group):
            low_copy(k, lax.rem(y + d, group), y).wait_recv()
        h, l = split(low_all[k].reshape(depth, width))
        low_s[0:depth, :] = h
        low_s[depth:, :] = l
        for n in range(steps):
            at = slice(n * wide, (n + 1) * wide)
            below = slice(n * wide, width)
            both = mm(low_s[:, below], diag_h[below, at])
            term = both[0:depth] + both[depth:] + mm(low_s[0:depth, below], diag_l[below, at])
            h, l = split(term)
            fold_h[k, :, at] = h
            fold_l[k, :, at] = l
        return carry

    lax.fori_loop(0, n_col - 1 - col, fold, 0)

    def x_copy(k, owner, to, to_col):
        return pltpu.make_async_remote_copy(
            src_ref=solved.at[:, pl.ds(pl.multiple_of(to * depth, depth), depth)],
            dst_ref=x_in.at[k, owner],
            send_sem=x_tx.at[to_col, to],
            recv_sem=x_rx.at[k, owner],
            device_id=(to * group + y, to_col),
            device_id_type=MESH,
        )

    def absorb(i, carry):
        k = n_col - 1 - i
        for d in range(n_z):
            x_copy(k, d, z, col).wait_recv()
        h, l = split(x_in[k].reshape(sub, depth))
        x_s[0:sub, :] = h
        x_s[sub:, :] = l
        for n in range(steps):
            at = slice(n * wide, (n + 1) * wide)
            both = mm(x_s[...], fold_h[k, :, at])
            term = both[0:sub] + both[sub:] + mm(x_s[0:sub, :], fold_l[k, :, at])
            acc[:, :, at] = acc[:, :, at] - term.reshape(n_z, share, wide)
        return carry

    lax.fori_loop(0, n_col - 1 - col, absorb, 0)

    def red_copy(owner, to):
        return pltpu.make_async_remote_copy(
            src_ref=acc.at[to],
            dst_ref=red_in.at[owner],
            send_sem=red_tx.at[to],
            recv_sem=red_rx.at[owner],
            device_id=(to * group + y, col),
            device_id_type=MESH,
        )

    for d in range(1, n_z):
        red_copy(z, lax.rem(z + d, n_z)).start()
    total = acc[z]
    for d in range(1, n_z):
        at = lax.rem(z + d, n_z)
        red_copy(at, z).wait_recv()
        total = total + red_in[at]
    solved[...] = total

    def spread(i, carry):
        to_col = col - 1 - i
        for d in range(n_z):
            x_copy(col, z, lax.rem(z + d, n_z), to_col).start()
        return carry

    lax.fori_loop(0, col, spread, 0)
    out_ref[...] = total

    def spread_done(i, carry):
        to_col = col - 1 - i
        for d in range(n_z):
            x_copy(col, z, lax.rem(z + d, n_z), to_col).wait_send()
        return carry

    lax.fori_loop(0, col, spread_done, 0)
    for d in range(1, n_z):
        red_copy(z, lax.rem(z + d, n_z)).wait_send()
    for d in range(1, group):
        part_copy(y, lax.rem(y + d, group)).wait_send()
    for e in range(1, n_col):
        sel_copy(col, others_col(e)).wait_send()
    for k in range(n_col - 1, 0, -1):

        @pl.when(col < k)
        def _():
            for d in range(1, group):
                low_copy(k, y, lax.rem(y + d, group)).wait_send()


def on_device(
    n_row, n_col, anc_factor, anc_solution, slot_row, tile_count, lower_factor, diag_inverse, rhs
):
    panels, rows_local, width = lower_factor.shape
    slots = slot_row.shape[0]
    share = rhs.shape[0]
    n_rhs = share * n_row
    group = max(2, LANES // rows_local)
    n_z = n_row // group
    depth = group * rows_local
    sub = share * n_z
    mine, parents = anc_solution.shape
    dma = pltpu.SemaphoreType.DMA
    vmem = pltpu.VMEM
    in_vmem = pl.BlockSpec(memory_space=pltpu.VMEM)
    anywhere = pl.BlockSpec(memory_space=pl.ANY)
    return pl.pallas_call(
        functools.partial(kernel, group, n_row, n_col),
        out_shape=jax.ShapeDtypeStruct(rhs.shape, F32),
        in_specs=[
            in_vmem,
            pl.BlockSpec(memory_space=pltpu.SMEM),
            in_vmem,
            in_vmem,
            anywhere,
            anywhere,
            anywhere,
        ],
        out_specs=in_vmem,
        scratch_shapes=[
            vmem((slots, width), F32),
            vmem((slots, width), BF16),
            vmem((slots, width), BF16),
            vmem((width, width), F32),
            vmem((width, width), BF16),
            vmem((width, width), BF16),
            vmem((panels, group, rows_local, width), F32),
            vmem((2 * depth, width), BF16),
            vmem((panels, depth, width), BF16),
            vmem((panels, depth, width), BF16),
            vmem((2 * mine, parents), BF16),
            vmem((n_col, mine, slots), F32),
            vmem((2 * n_rhs, slots), BF16),
            vmem((group, n_z, share, width), F32),
            vmem((group, n_z, share, width), F32),
            vmem((2 * sub, width), BF16),
            vmem((n_z, share, width), F32),
            vmem((n_z, share, width), F32),
            vmem((share, width), F32),
            vmem((panels, n_z, share, depth), F32),
            vmem((2 * sub, depth), BF16),
            dma,
            dma,
            dma((panels,)),
            dma((n_col,)),
            dma((n_col,)),
            dma((panels, group)),
            dma((panels, group)),
            dma((group,)),
            dma((group,)),
            dma((n_z,)),
            dma((n_z,)),
            dma((n_col, n_z)),
            dma((panels, n_z)),
        ],
        compiler_params=pltpu.CompilerParams(
            collective_id=0, has_side_effects=True, vmem_limit_bytes=52 * 1024 * 1024
        ),
        name="front_solve",
    )(slot_row[None, :], tile_count, anc_solution, rhs, anc_factor, lower_factor, diag_inverse)


def solution(mesh):
    in_specs = (
        P("row", "col"),
        P("col", "row"),
        P("row"),
        P("row"),
        P(None, "row", "col"),
        P("col", None, None),
        P("row", "col"),
    )
    body = functools.partial(on_device, mesh.shape["row"], mesh.shape["col"])
    return jax.shard_map(
        body, mesh=mesh, in_specs=in_specs, out_specs=P("row", "col"), check_vma=False
    )
```

```python
import functools

import jax
import jax.numpy as jnp
from jax import lax
from jax.experimental import pallas as pl
from jax.experimental.pallas import tpu as pltpu
from jax.sharding import PartitionSpec as P

TILE = 128
LANES = 128
MESH = pl.DeviceIdType.MESH
F32 = jnp.float32
BF16 = jnp.bfloat16


def split(x):
    hi = x.astype(BF16)
    lo = (x - hi.astype(F32)).astype(BF16)
    return hi, lo


def mm(a, b):
    return jnp.dot(a, b, preferred_element_type=F32)


def kernel(
    group,
    n_row,
    n_col,
    count_ref,
    slot_hbm,
    parent_hbm,
    rhs_hbm,
    anc_ref,
    low_ref,
    diag_ref,
    out_ref,
    slot_ref,
    parent_ref,
    rhs_ref,
    anc_f,
    anc_h,
    anc_l,
    diag_f,
    diag_h,
    diag_l,
    low_all,
    low_s,
    fold_h,
    fold_l,
    par_s,
    sel,
    sel_s,
    part,
    part_in,
    pre_s,
    acc,
    red_in,
    solved,
    x_in,
    x_s,
    sem_in,
    sem_anc,
    sem_diag,
    sem_low,
    sel_tx,
    fwd_tx,
    sel_rx,
    low_tx,
    low_rx,
    part_tx,
    part_rx,
    red_tx,
    red_rx,
    x_tx,
    x_rx,
):
    row = lax.axis_index("row")
    col = lax.axis_index("col")
    n_z = n_row // group
    z = row // group
    y = row % group
    width = diag_f.shape[1]
    slots = sel.shape[2]
    share = rhs_ref.shape[0]
    n_rhs = share * n_row
    sub = share * n_z
    wide = min(256, width)
    steps = width // wide
    depth = x_in.shape[3]

    copy_slot = pltpu.make_async_copy(slot_hbm, slot_ref, sem_in.at[0])
    copy_slot.start()
    copy_parent = pltpu.make_async_copy(parent_hbm, parent_ref, sem_in.at[1])
    copy_parent.start()
    copy_rhs = pltpu.make_async_copy(rhs_hbm, rhs_ref, sem_in.at[2])
    copy_rhs.start()
    copy_anc = pltpu.make_async_copy(anc_ref, anc_f, sem_anc)
    copy_anc.start()
    copy_diag = pltpu.make_async_copy(diag_ref.at[0], diag_f, sem_diag)
    copy_diag.start()
    for k in range(1, n_col):
        pltpu.make_async_copy(low_ref.at[k], low_all.at[k, y], sem_low.at[k]).start()

    barrier = pltpu.get_barrier_semaphore()

    def greet(dev_row, dev_col):
        pl.semaphore_signal(barrier, inc=1, device_id=(dev_row, dev_col), device_id_type=MESH)

    for d in range(n_z):
        for e in range(n_col):
            if d or e:
                greet(lax.rem(z + d, n_z) * group + y, lax.rem(col + e, n_col))
    for d in range(1, group):
        greet(z * group + lax.rem(y + d, group), col)

    mine = sel.shape[1]
    picks = slots // wide
    core = lax.rem(col, 2)
    sibling = col + 1 - 2 * core

    def sel_copy(owner, n, to, tx):
        at = slice(n * wide, (n + 1) * wide)
        return pltpu.make_async_remote_copy(
            src_ref=sel.at[owner, :, at],
            dst_ref=sel.at[owner, :, at],
            send_sem=tx,
            recv_sem=sel_rx.at[owner, n],
            device_id=(row, to),
            device_id_type=MESH,
        )

    def far_col(e):
        return lax.rem(col + 2 * e, n_col)

    far = n_col // 2
    copy_slot.wait()
    copy_parent.wait()
    hi, lo = split(parent_ref[...])
    par_s[0:mine, :] = hi
    par_s[mine:, :] = lo
    parents = parent_ref.shape[1]
    for n in range(picks):
        at = slice(n * wide, (n + 1) * wide)
        place = lax.broadcasted_iota(jnp.int32, (1, wide), 1) + n * wide
        wanted = jnp.where(place < count_ref[0] * TILE, slot_ref[:, at], -1)
        which = lax.broadcasted_iota(jnp.int32, (parents, wide), 0)
        hot = jnp.where(which == wanted, 1.0, 0.0).astype(BF16)
        both = mm(par_s[...], hot)
        sel[col, :, at] = both[0:mine] + both[mine:]
        if n == 0:
            pl.semaphore_wait(barrier, n_z * n_col - 1 + group - 1)
        for e in range(1, far):
            sel_copy(col, n, far_col(e), sel_tx.at[far_col(e), n]).start()
        sel_copy(col, n, sibling, sel_tx.at[sibling, n]).start()

    def low_copy(k, owner, to):
        return pltpu.make_async_remote_copy(
            src_ref=low_ref.at[k],
            dst_ref=low_all.at[k, owner],
            send_sem=low_tx.at[k, to],
            recv_sem=low_rx.at[k, owner],
            device_id=(z * group + to, col),
            device_id_type=MESH,
        )

    for k in range(n_col - 1, 0, -1):

        @pl.when(col < k)
        def _():
            for d in range(1, group):
                low_copy(k, y, lax.rem(y + d, group)).start()

    def split_rows(src, dst_h, dst_l):
        rows = 128

        def body(i, carry):
            at = pl.ds(pl.multiple_of(i * rows, rows), rows)
            h, l = split(src[at, :])
            dst_h[at, :] = h
            dst_l[at, :] = l
            return carry

        lax.fori_loop(0, src.shape[0] // rows, body, 0)

    copy_anc.wait()
    split_rows(anc_f, anc_h, anc_l)
    for n in range(picks):
        for e in range(1, far):
            owner = far_col(e)
            sel_copy(owner, n, col, sel_tx.at[col, n]).wait_recv()
            sel_copy(owner, n, sibling, fwd_tx.at[owner, n]).start()
    copy_diag.wait()
    split_rows(diag_f, diag_h, diag_l)
    for n in range(picks):
        for e in range(far):
            owner = lax.rem(sibling + 2 * e, n_col)
            sel_copy(owner, n, col, sel_tx.at[col, n]).wait_recv()
    hi, lo = split(sel[...].reshape(n_rhs, slots))
    sel_s[0:n_rhs, :] = hi
    sel_s[n_rhs:, :] = lo
    def part_copy(owner, to, n):
        at = slice(n * wide, (n + 1) * wide)
        return pltpu.make_async_remote_copy(
            src_ref=part.at[to, :, :, at],
            dst_ref=part_in.at[owner, :, :, at],
            send_sem=part_tx.at[to, n],
            recv_sem=part_rx.at[owner, n],
            device_id=(z * group + to, col),
            device_id_type=MESH,
        )

    def red_copy(owner, to, n):
        at = slice(n * wide, (n + 1) * wide)
        return pltpu.make_async_remote_copy(
            src_ref=acc.at[to, :, at],
            dst_ref=red_in.at[owner, :, at],
            send_sem=red_tx.at[to, n],
            recv_sem=red_rx.at[owner, n],
            device_id=(to * group + y, col),
            device_id_type=MESH,
        )

    def send_sums(n):
        for d in range(1, n_z):
            red_copy(z, lax.rem(z + d, n_z), n).start()

    order = range(steps - 1, -1, -1)
    for n in order:
        at = slice(n * wide, (n + 1) * wide)
        both = mm(sel_s[...], anc_h[:, at])
        term = both[0:n_rhs] + both[n_rhs:] + mm(sel_s[0:n_rhs, :], anc_l[:, at])
        for r in range(n_row):
            part[r % group, r // group, :, at] = term[r * share : (r + 1) * share]
        for d in range(1, group):
            part_copy(y, lax.rem(y + d, group), n).start()

    copy_rhs.wait()
    zs = lax.broadcasted_iota(jnp.int32, (n_z, 1, 1), 0)
    for n in order:
        at = slice(n * wide, (n + 1) * wide)
        below = slice(n * wide, width)
        pre = jnp.where(zs == z, rhs_ref[:, at][None], 0.0) - part[y, :, :, at]
        for d in range(1, group):
            owner = lax.rem(y + d, group)
            part_copy(owner, y, n).wait_recv()
            pre = pre - part_in[owner, :, :, at]
        hi, lo = split(pre.reshape(sub, wide))
        pre_s[0:sub, at] = hi
        pre_s[sub:, at] = lo
        both = mm(pre_s[:, below], diag_h[below, at])
        term = both[0:sub] + both[sub:] + mm(pre_s[0:sub, below], diag_l[below, at])
        acc[:, :, at] = term.reshape(n_z, share, wide)

        @pl.when(col == n_col - 1)
        def _():
            send_sums(n)

    for k in range(1, n_col):
        pltpu.make_async_copy(low_ref.at[k], low_all.at[k, y], sem_low.at[k]).wait()

    def fold(i, carry):
        k = n_col - 1 - i
        for d in range(1, group):
            low_copy(k, lax.rem(y + d, group), y).wait_recv()
        h, l = split(low_all[k].reshape(depth, width))
        low_s[0:depth, :] = h
        low_s[depth:, :] = l
        for n in range(steps):
            at = slice(n * wide, (n + 1) * wide)
            below = slice(n * wide, width)
            both = mm(low_s[:, below], diag_h[below, at])
            term = both[0:depth] + both[depth:] + mm(low_s[0:depth, below], diag_l[below, at])
            h, l = split(term)
            fold_h[k, :, at] = h
            fold_l[k, :, at] = l
        return carry

    lax.fori_loop(0, n_col - 1 - col, fold, 0)

    def x_copy(k, owner, to, to_col):
        return pltpu.make_async_remote_copy(
            src_ref=solved.at[:, pl.ds(pl.multiple_of(to * depth, depth), depth)],
            dst_ref=x_in.at[k, owner],
            send_sem=x_tx.at[to_col, to],
            recv_sem=x_rx.at[k, owner],
            device_id=(to * group + y, to_col),
            device_id_type=MESH,
        )

    def absorb(i, carry):
        k = n_col - 1 - i
        for d in range(n_z):
            x_copy(k, d, z, col).wait_recv()
        h, l = split(x_in[k].reshape(sub, depth))
        x_s[0:sub, :] = h
        x_s[sub:, :] = l
        for n in order:
            at = slice(n * wide, (n + 1) * wide)
            both = mm(x_s[...], fold_h[k, :, at])
            term = both[0:sub] + both[sub:] + mm(x_s[0:sub, :], fold_l[k, :, at])
            acc[:, :, at] = acc[:, :, at] - term.reshape(n_z, share, wide)

            @pl.when(k == col + 1)
            def _():
                send_sums(n)

        return carry

    lax.fori_loop(0, n_col - 1 - col, absorb, 0)

    per = wide // depth
    for n in order:
        at = slice(n * wide, (n + 1) * wide)
        total = acc[z, :, at]
        for d in range(1, n_z):
            owner = lax.rem(z + d, n_z)
            red_copy(owner, z, n).wait_recv()
            total = total + red_in[owner, :, at]
        solved[:, at] = total

        @pl.when(col > 0)
        def _():
            for to in range(n * per, (n + 1) * per):
                x_copy(col, z, to, col - 1).start()

    def spread(i, carry):
        for to in range(n_z):
            x_copy(col, z, to, col - 2 - i).start()
        return carry

    lax.fori_loop(0, col - 1, spread, 0)
    out_ref[...] = solved[...]

    def spread_done(i, carry):
        for to in range(n_z):
            x_copy(col, z, to, col - 1 - i).wait_send()
        return carry

    lax.fori_loop(0, col, spread_done, 0)
    for n in range(steps):
        for d in range(1, n_z):
            red_copy(z, lax.rem(z + d, n_z), n).wait_send()
        for d in range(1, group):
            part_copy(y, lax.rem(y + d, group), n).wait_send()
    for n in range(picks):
        for e in range(1, far):
            owner = far_col(e)
            sel_copy(col, n, owner, sel_tx.at[owner, n]).wait_send()
            sel_copy(owner, n, sibling, fwd_tx.at[owner, n]).wait_send()
        sel_copy(col, n, sibling, sel_tx.at[sibling, n]).wait_send()
    for k in range(n_col - 1, 0, -1):

        @pl.when(col < k)
        def _():
            for d in range(1, group):
                low_copy(k, y, lax.rem(y + d, group)).wait_send()


def on_device(
    n_row, n_col, anc_factor, anc_solution, slot_row, tile_count, lower_factor, diag_inverse, rhs
):
    panels, rows_local, width = lower_factor.shape
    slots = slot_row.shape[0]
    share = rhs.shape[0]
    n_rhs = share * n_row
    group = max(2, LANES // rows_local)
    n_z = n_row // group
    depth = group * rows_local
    sub = share * n_z
    mine, parents = anc_solution.shape
    wide = min(256, width)
    picks, steps = slots // wide, width // wide
    dma = pltpu.SemaphoreType.DMA
    vmem = pltpu.VMEM
    in_vmem = pl.BlockSpec(memory_space=pltpu.VMEM)
    anywhere = pl.BlockSpec(memory_space=pl.ANY)
    return pl.pallas_call(
        functools.partial(kernel, group, n_row, n_col),
        out_shape=jax.ShapeDtypeStruct(rhs.shape, F32),
        in_specs=[
            pl.BlockSpec(memory_space=pltpu.SMEM),
            anywhere,
            anywhere,
            anywhere,
            anywhere,
            anywhere,
            anywhere,
        ],
        out_specs=in_vmem,
        scratch_shapes=[
            vmem((1, slots), jnp.int32),
            vmem((mine, parents), F32),
            vmem(rhs.shape, F32),
            vmem((slots, width), F32),
            vmem((slots, width), BF16),
            vmem((slots, width), BF16),
            vmem((width, width), F32),
            vmem((width, width), BF16),
            vmem((width, width), BF16),
            vmem((panels, group, rows_local, width), F32),
            vmem((2 * depth, width), BF16),
            vmem((panels, depth, width), BF16),
            vmem((panels, depth, width), BF16),
            vmem((2 * mine, parents), BF16),
            vmem((n_col, mine, slots), F32),
            vmem((2 * n_rhs, slots), BF16),
            vmem((group, n_z, share, width), F32),
            vmem((group, n_z, share, width), F32),
            vmem((2 * sub, width), BF16),
            vmem((n_z, share, width), F32),
            vmem((n_z, share, width), F32),
            vmem((share, width), F32),
            vmem((panels, n_z, share, depth), F32),
            vmem((2 * sub, depth), BF16),
            dma((3,)),
            dma,
            dma,
            dma((panels,)),
            dma((n_col, picks)),
            dma((n_col, picks)),
            dma((n_col, picks)),
            dma((panels, group)),
            dma((panels, group)),
            dma((group, steps)),
            dma((group, steps)),
            dma((n_z, steps)),
            dma((n_z, steps)),
            dma((n_col, n_z)),
            dma((panels, n_z)),
        ],
        compiler_params=pltpu.CompilerParams(
            collective_id=0, has_side_effects=True, vmem_limit_bytes=52 * 1024 * 1024
        ),
        name="front_solve",
    )(tile_count, slot_row[None, :], anc_solution, rhs, anc_factor, lower_factor, diag_inverse)


def solution(mesh):
    in_specs = (
        P("row", "col"),
        P("col", "row"),
        P("row"),
        P("row"),
        P(None, "row", "col"),
        P("col", None, None),
        P("row", "col"),
    )
    body = functools.partial(on_device, mesh.shape["row"], mesh.shape["col"])
    return jax.shard_map(
        body, mesh=mesh, in_specs=in_specs, out_specs=P("row", "col"), check_vma=False
    )
```

```python
import functools

import jax
import jax.numpy as jnp
from jax import lax
from jax.experimental import pallas as pl
from jax.experimental.pallas import tpu as pltpu
from jax.sharding import PartitionSpec as P

TILE = 128
LANES = 128
MESH = pl.DeviceIdType.MESH
F32 = jnp.float32
BF16 = jnp.bfloat16


def split(x):
    hi = x.astype(BF16)
    lo = (x - hi.astype(F32)).astype(BF16)
    return hi, lo


def mm(a, b):
    return jnp.dot(a, b, preferred_element_type=F32)


def kernel(
    group,
    n_row,
    n_col,
    count_ref,
    slot_hbm,
    parent_hbm,
    rhs_hbm,
    anc_ref,
    low_ref,
    diag_ref,
    out_ref,
    slot_ref,
    parent_ref,
    rhs_ref,
    anc_f,
    anc_h,
    anc_l,
    diag_f,
    diag_h,
    diag_l,
    low_all,
    low_s,
    fold_h,
    fold_l,
    par_s,
    sel,
    sel_s,
    part,
    part_in,
    pre_s,
    acc,
    red_in,
    solved,
    x_in,
    x_s,
    sem_in,
    sem_anc,
    sem_diag,
    sem_low,
    sel_tx,
    fwd_tx,
    sel_rx,
    low_tx,
    low_rx,
    part_tx,
    part_rx,
    red_tx,
    red_rx,
    x_tx,
    x_rx,
):
    row = lax.axis_index("row")
    col = lax.axis_index("col")
    n_z = n_row // group
    z = row // group
    y = row % group
    width = diag_f.shape[1]
    slots = sel.shape[2]
    share = rhs_ref.shape[0]
    n_rhs = share * n_row
    sub = share * n_z
    wide = min(256, width)
    steps = width // wide
    depth = x_in.shape[3]

    copy_slot = pltpu.make_async_copy(slot_hbm, slot_ref, sem_in.at[0])
    copy_slot.start()
    copy_parent = pltpu.make_async_copy(parent_hbm, parent_ref, sem_in.at[1])
    copy_parent.start()
    copy_rhs = pltpu.make_async_copy(rhs_hbm, rhs_ref, sem_in.at[2])
    copy_rhs.start()
    copy_anc = pltpu.make_async_copy(anc_ref, anc_f, sem_anc)
    copy_anc.start()
    copy_diag = pltpu.make_async_copy(diag_ref.at[0], diag_f, sem_diag)
    copy_diag.start()
    for k in range(1, n_col):
        pltpu.make_async_copy(low_ref.at[k], low_all.at[k, y], sem_low.at[k]).start()

    barrier = pltpu.get_barrier_semaphore()

    def greet(dev_row, dev_col):
        pl.semaphore_signal(barrier, inc=1, device_id=(dev_row, dev_col), device_id_type=MESH)

    for d in range(n_z):
        for e in range(n_col):
            if d or e:
                greet(lax.rem(z + d, n_z) * group + y, lax.rem(col + e, n_col))
    for d in range(1, group):
        greet(z * group + lax.rem(y + d, group), col)

    pl.semaphore_wait(barrier, n_z * n_col - 1 + group - 1)

    def low_copy(k, owner, to):
        return pltpu.make_async_remote_copy(
            src_ref=low_ref.at[k],
            dst_ref=low_all.at[k, owner],
            send_sem=low_tx.at[k, to],
            recv_sem=low_rx.at[k, owner],
            device_id=(z * group + to, col),
            device_id_type=MESH,
        )

    for k in range(n_col - 1, 0, -1):

        @pl.when(col < k)
        def _():
            for d in range(1, group):
                low_copy(k, y, lax.rem(y + d, group)).start()

    mine = sel.shape[1]
    picks = slots // wide
    core = lax.rem(col, 2)
    sibling = col + 1 - 2 * core

    def sel_copy(owner, n, to, tx):
        at = slice(n * wide, (n + 1) * wide)
        return pltpu.make_async_remote_copy(
            src_ref=sel.at[owner, :, at],
            dst_ref=sel.at[owner, :, at],
            send_sem=tx,
            recv_sem=sel_rx.at[owner, n],
            device_id=(row, to),
            device_id_type=MESH,
        )

    def far_col(e):
        return lax.rem(col + 2 * e, n_col)

    far = n_col // 2
    copy_slot.wait()
    copy_parent.wait()
    hi, lo = split(parent_ref[...])
    par_s[0:mine, :] = hi
    par_s[mine:, :] = lo
    parents = parent_ref.shape[1]
    for n in range(picks):
        at = slice(n * wide, (n + 1) * wide)
        place = lax.broadcasted_iota(jnp.int32, (1, wide), 1) + n * wide
        wanted = jnp.where(place < count_ref[0] * TILE, slot_ref[:, at], -1)
        which = lax.broadcasted_iota(jnp.int32, (parents, wide), 0)
        hot = jnp.where(which == wanted, 1.0, 0.0).astype(BF16)
        both = mm(par_s[...], hot)
        sel[col, :, at] = both[0:mine] + both[mine:]
        for e in range(1, far):
            sel_copy(col, n, far_col(e), sel_tx.at[far_col(e), n]).start()
        sel_copy(col, n, sibling, sel_tx.at[sibling, n]).start()

    def split_rows(src, dst_h, dst_l):
        rows = 128

        def body(i, carry):
            at = pl.ds(pl.multiple_of(i * rows, rows), rows)
            h, l = split(src[at, :])
            dst_h[at, :] = h
            dst_l[at, :] = l
            return carry

        lax.fori_loop(0, src.shape[0] // rows, body, 0)

    copy_anc.wait()
    split_rows(anc_f, anc_h, anc_l)
    for n in range(picks):
        for e in range(1, far):
            owner = far_col(e)
            sel_copy(owner, n, col, sel_tx.at[col, n]).wait_recv()
            sel_copy(owner, n, sibling, fwd_tx.at[owner, n]).start()
    copy_diag.wait()
    split_rows(diag_f, diag_h, diag_l)
    for n in range(picks):
        for e in range(far):
            owner = lax.rem(sibling + 2 * e, n_col)
            sel_copy(owner, n, col, sel_tx.at[col, n]).wait_recv()
    hi, lo = split(sel[...].reshape(n_rhs, slots))
    sel_s[0:n_rhs, :] = hi
    sel_s[n_rhs:, :] = lo
    def part_copy(owner, to, n):
        at = slice(n * wide, (n + 1) * wide)
        return pltpu.make_async_remote_copy(
            src_ref=part.at[to, :, :, at],
            dst_ref=part_in.at[owner, :, :, at],
            send_sem=part_tx.at[to, n],
            recv_sem=part_rx.at[owner, n],
            device_id=(z * group + to, col),
            device_id_type=MESH,
        )

    def red_copy(owner, to, n):
        at = slice(n * wide, (n + 1) * wide)
        return pltpu.make_async_remote_copy(
            src_ref=acc.at[to, :, at],
            dst_ref=red_in.at[owner, :, at],
            send_sem=red_tx.at[to, n],
            recv_sem=red_rx.at[owner, n],
            device_id=(to * group + y, col),
            device_id_type=MESH,
        )

    def send_sums(n):
        for d in range(1, n_z):
            red_copy(z, lax.rem(z + d, n_z), n).start()

    order = range(steps - 1, -1, -1)
    for n in order:
        at = slice(n * wide, (n + 1) * wide)
        both = mm(sel_s[...], anc_h[:, at])
        term = both[0:n_rhs] + both[n_rhs:] + mm(sel_s[0:n_rhs, :], anc_l[:, at])
        for r in range(n_row):
            part[r % group, r // group, :, at] = term[r * share : (r + 1) * share]
        for d in range(1, group):
            part_copy(y, lax.rem(y + d, group), n).start()

    copy_rhs.wait()
    zs = lax.broadcasted_iota(jnp.int32, (n_z, 1, 1), 0)
    for n in order:
        at = slice(n * wide, (n + 1) * wide)
        below = slice(n * wide, width)
        pre = jnp.where(zs == z, rhs_ref[:, at][None], 0.0) - part[y, :, :, at]
        for d in range(1, group):
            owner = lax.rem(y + d, group)
            part_copy(owner, y, n).wait_recv()
            pre = pre - part_in[owner, :, :, at]
        hi, lo = split(pre.reshape(sub, wide))
        pre_s[0:sub, at] = hi
        pre_s[sub:, at] = lo
        both = mm(pre_s[:, below], diag_h[below, at])
        term = both[0:sub] + both[sub:] + mm(pre_s[0:sub, below], diag_l[below, at])
        acc[:, :, at] = term.reshape(n_z, share, wide)

        @pl.when(col == n_col - 1)
        def _():
            send_sums(n)

    for k in range(1, n_col):
        pltpu.make_async_copy(low_ref.at[k], low_all.at[k, y], sem_low.at[k]).wait()

    def fold(i, carry):
        k = n_col - 1 - i
        for d in range(1, group):
            low_copy(k, lax.rem(y + d, group), y).wait_recv()
        h, l = split(low_all[k].reshape(depth, width))
        low_s[0:depth, :] = h
        low_s[depth:, :] = l
        for n in range(steps):
            at = slice(n * wide, (n + 1) * wide)
            below = slice(n * wide, width)
            both = mm(low_s[:, below], diag_h[below, at])
            term = both[0:depth] + both[depth:] + mm(low_s[0:depth, below], diag_l[below, at])
            h, l = split(term)
            fold_h[k, :, at] = h
            fold_l[k, :, at] = l
        return carry

    lax.fori_loop(0, n_col - 1 - col, fold, 0)

    def x_copy(k, owner, to, to_col):
        return pltpu.make_async_remote_copy(
            src_ref=solved.at[:, pl.ds(pl.multiple_of(to * depth, depth), depth)],
            dst_ref=x_in.at[k, owner],
            send_sem=x_tx.at[to_col, to],
            recv_sem=x_rx.at[k, owner],
            device_id=(to * group + y, to_col),
            device_id_type=MESH,
        )

    def absorb(i, carry):
        k = n_col - 1 - i
        for d in range(n_z):
            x_copy(k, d, z, col).wait_recv()
        h, l = split(x_in[k].reshape(sub, depth))
        x_s[0:sub, :] = h
        x_s[sub:, :] = l
        for n in order:
            at = slice(n * wide, (n + 1) * wide)
            both = mm(x_s[...], fold_h[k, :, at])
            term = both[0:sub] + both[sub:] + mm(x_s[0:sub, :], fold_l[k, :, at])
            acc[:, :, at] = acc[:, :, at] - term.reshape(n_z, share, wide)

            @pl.when(k == col + 1)
            def _():
                send_sums(n)

        return carry

    lax.fori_loop(0, n_col - 1 - col, absorb, 0)

    per = wide // depth
    for n in order:
        at = slice(n * wide, (n + 1) * wide)
        total = acc[z, :, at]
        for d in range(1, n_z):
            owner = lax.rem(z + d, n_z)
            red_copy(owner, z, n).wait_recv()
            total = total + red_in[owner, :, at]
        solved[:, at] = total

        @pl.when(col > 0)
        def _():
            for to in range(n * per, (n + 1) * per):
                x_copy(col, z, to, col - 1).start()

    def spread(i, carry):
        for to in range(n_z):
            x_copy(col, z, to, col - 2 - i).start()
        return carry

    lax.fori_loop(0, col - 1, spread, 0)
    out_ref[...] = solved[...]

    def spread_done(i, carry):
        for to in range(n_z):
            x_copy(col, z, to, col - 1 - i).wait_send()
        return carry

    lax.fori_loop(0, col, spread_done, 0)
    for n in range(steps):
        for d in range(1, n_z):
            red_copy(z, lax.rem(z + d, n_z), n).wait_send()
        for d in range(1, group):
            part_copy(y, lax.rem(y + d, group), n).wait_send()
    for n in range(picks):
        for e in range(1, far):
            owner = far_col(e)
            sel_copy(col, n, owner, sel_tx.at[owner, n]).wait_send()
            sel_copy(owner, n, sibling, fwd_tx.at[owner, n]).wait_send()
        sel_copy(col, n, sibling, sel_tx.at[sibling, n]).wait_send()
    for k in range(n_col - 1, 0, -1):

        @pl.when(col < k)
        def _():
            for d in range(1, group):
                low_copy(k, y, lax.rem(y + d, group)).wait_send()


def on_device(
    n_row, n_col, anc_factor, anc_solution, slot_row, tile_count, lower_factor, diag_inverse, rhs
):
    panels, rows_local, width = lower_factor.shape
    slots = slot_row.shape[0]
    share = rhs.shape[0]
    n_rhs = share * n_row
    group = max(2, LANES // rows_local)
    n_z = n_row // group
    depth = group * rows_local
    sub = share * n_z
    mine, parents = anc_solution.shape
    wide = min(256, width)
    picks, steps = slots // wide, width // wide
    dma = pltpu.SemaphoreType.DMA
    vmem = pltpu.VMEM
    in_vmem = pl.BlockSpec(memory_space=pltpu.VMEM)
    anywhere = pl.BlockSpec(memory_space=pl.ANY)
    return pl.pallas_call(
        functools.partial(kernel, group, n_row, n_col),
        out_shape=jax.ShapeDtypeStruct(rhs.shape, F32),
        in_specs=[
            pl.BlockSpec(memory_space=pltpu.SMEM),
            anywhere,
            anywhere,
            anywhere,
            anywhere,
            anywhere,
            anywhere,
        ],
        out_specs=in_vmem,
        scratch_shapes=[
            vmem((1, slots), jnp.int32),
            vmem((mine, parents), F32),
            vmem(rhs.shape, F32),
            vmem((slots, width), F32),
            vmem((slots, width), BF16),
            vmem((slots, width), BF16),
            vmem((width, width), F32),
            vmem((width, width), BF16),
            vmem((width, width), BF16),
            vmem((panels, group, rows_local, width), F32),
            vmem((2 * depth, width), BF16),
            vmem((panels, depth, width), BF16),
            vmem((panels, depth, width), BF16),
            vmem((2 * mine, parents), BF16),
            vmem((n_col, mine, slots), F32),
            vmem((2 * n_rhs, slots), BF16),
            vmem((group, n_z, share, width), F32),
            vmem((group, n_z, share, width), F32),
            vmem((2 * sub, width), BF16),
            vmem((n_z, share, width), F32),
            vmem((n_z, share, width), F32),
            vmem((share, width), F32),
            vmem((panels, n_z, share, depth), F32),
            vmem((2 * sub, depth), BF16),
            dma((3,)),
            dma,
            dma,
            dma((panels,)),
            dma((n_col, picks)),
            dma((n_col, picks)),
            dma((n_col, picks)),
            dma((panels, group)),
            dma((panels, group)),
            dma((group, steps)),
            dma((group, steps)),
            dma((n_z, steps)),
            dma((n_z, steps)),
            dma((n_col, n_z)),
            dma((panels, n_z)),
        ],
        compiler_params=pltpu.CompilerParams(
            collective_id=0, has_side_effects=True, vmem_limit_bytes=52 * 1024 * 1024
        ),
        name="front_solve",
    )(tile_count, slot_row[None, :], anc_solution, rhs, anc_factor, lower_factor, diag_inverse)


def solution(mesh):
    in_specs = (
        P("row", "col"),
        P("col", "row"),
        P("row"),
        P("row"),
        P(None, "row", "col"),
        P("col", None, None),
        P("row", "col"),
    )
    body = functools.partial(on_device, mesh.shape["row"], mesh.shape["col"])
    return jax.shard_map(
        body, mesh=mesh, in_specs=in_specs, out_specs=P("row", "col"), check_vma=False
    )
```

```python
import functools

import jax
import jax.numpy as jnp
from jax import lax
from jax.experimental import pallas as pl
from jax.experimental.pallas import tpu as pltpu
from jax.sharding import PartitionSpec as P

TILE = 128
LANES = 128
MESH = pl.DeviceIdType.MESH
F32 = jnp.float32
BF16 = jnp.bfloat16


def split(x):
    hi = x.astype(BF16)
    lo = (x - hi.astype(F32)).astype(BF16)
    return hi, lo


def mm(a, b):
    return jnp.dot(a, b, preferred_element_type=F32)


def kernel(
    group,
    n_row,
    n_col,
    slot_ref,
    count_ref,
    parent_ref,
    rhs_ref,
    anc_ref,
    low_ref,
    diag_ref,
    out_ref,
    anc_f,
    anc_h,
    anc_l,
    diag_f,
    diag_h,
    diag_l,
    low_all,
    low_s,
    fold_h,
    fold_l,
    par_s,
    sel,
    sel_s,
    part,
    part_in,
    pre_s,
    acc,
    red_in,
    solved,
    x_in,
    x_s,
    sem_anc,
    sem_diag,
    sem_low,
    sel_tx,
    sel_rx,
    low_tx,
    low_rx,
    part_tx,
    part_rx,
    red_tx,
    red_rx,
    x_tx,
    x_rx,
):
    row = lax.axis_index("row")
    col = lax.axis_index("col")
    n_z = n_row // group
    z = row // group
    y = row % group
    width = diag_f.shape[1]
    slots = sel.shape[2]
    share = rhs_ref.shape[0]
    n_rhs = share * n_row
    sub = share * n_z
    wide = min(256, width)
    steps = width // wide
    depth = x_in.shape[3]

    copy_anc = pltpu.make_async_copy(anc_ref, anc_f, sem_anc)
    copy_anc.start()
    copy_diag = pltpu.make_async_copy(diag_ref.at[0], diag_f, sem_diag)
    copy_diag.start()
    for k in range(1, n_col):
        pltpu.make_async_copy(low_ref.at[k], low_all.at[k, y], sem_low.at[k]).start()

    barrier = pltpu.get_barrier_semaphore()

    def greet(dev_row, dev_col):
        pl.semaphore_signal(barrier, inc=1, device_id=(dev_row, dev_col), device_id_type=MESH)

    for d in range(n_z):
        for e in range(n_col):
            if d or e:
                greet(lax.rem(z + d, n_z) * group + y, lax.rem(col + e, n_col))
    for d in range(1, group):
        greet(z * group + lax.rem(y + d, group), col)

    pl.semaphore_wait(barrier, n_z * n_col - 1 + group - 1)

    def low_copy(k, owner, to):
        return pltpu.make_async_remote_copy(
            src_ref=low_ref.at[k],
            dst_ref=low_all.at[k, owner],
            send_sem=low_tx.at[k, to],
            recv_sem=low_rx.at[k, owner],
            device_id=(z * group + to, col),
            device_id_type=MESH,
        )

    for k in range(n_col - 1, 0, -1):

        @pl.when(col < k)
        def _():
            for d in range(1, group):
                low_copy(k, y, lax.rem(y + d, group)).start()

    mine = sel.shape[1]
    hi, lo = split(parent_ref[...])
    par_s[0:mine, :] = hi
    par_s[mine:, :] = lo
    parents = parent_ref.shape[1]

    def select(n, carry):
        at = pl.ds(pl.multiple_of(n * wide, wide), wide)
        place = lax.broadcasted_iota(jnp.int32, (1, wide), 1) + n * wide
        wanted = jnp.where(place < count_ref[0] * TILE, slot_ref[:, at], -1)
        which = lax.broadcasted_iota(jnp.int32, (parents, wide), 0)
        hot = jnp.where(which == wanted, 1.0, 0.0).astype(BF16)
        both = mm(par_s[...], hot)
        sel[col, :, at] = both[0:mine] + both[mine:]
        return carry

    lax.fori_loop(0, slots // wide, select, 0)

    def sel_copy(owner, to):
        return pltpu.make_async_remote_copy(
            src_ref=sel.at[owner],
            dst_ref=sel.at[owner],
            send_sem=sel_tx.at[to],
            recv_sem=sel_rx.at[owner],
            device_id=(row, to),
            device_id_type=MESH,
        )

    def others_col(e):
        return lax.rem(col + e, n_col)

    for e in range(1, n_col):
        sel_copy(col, others_col(e)).start()

    def split_rows(src, dst_h, dst_l):
        rows = 128

        def body(i, carry):
            at = pl.ds(pl.multiple_of(i * rows, rows), rows)
            h, l = split(src[at, :])
            dst_h[at, :] = h
            dst_l[at, :] = l
            return carry

        lax.fori_loop(0, src.shape[0] // rows, body, 0)

    copy_anc.wait()
    split_rows(anc_f, anc_h, anc_l)

    for e in range(1, n_col):
        sel_copy(others_col(e), col).wait_recv()
    hi, lo = split(sel[...].reshape(n_rhs, slots))
    sel_s[0:n_rhs, :] = hi
    sel_s[n_rhs:, :] = lo
    for n in range(steps):
        at = slice(n * wide, (n + 1) * wide)
        both = mm(sel_s[...], anc_h[:, at])
        term = both[0:n_rhs] + both[n_rhs:] + mm(sel_s[0:n_rhs, :], anc_l[:, at])
        for r in range(n_row):
            part[r % group, r // group, :, at] = term[r * share : (r + 1) * share]

    def part_copy(owner, to):
        return pltpu.make_async_remote_copy(
            src_ref=part.at[to],
            dst_ref=part_in.at[owner],
            send_sem=part_tx.at[to],
            recv_sem=part_rx.at[owner],
            device_id=(z * group + to, col),
            device_id_type=MESH,
        )

    for d in range(1, group):
        part_copy(y, lax.rem(y + d, group)).start()

    copy_diag.wait()
    split_rows(diag_f, diag_h, diag_l)

    for d in range(1, group):
        part_copy(lax.rem(y + d, group), y).wait_recv()

    pre = part[y]
    for d in range(1, group):
        pre = pre + part_in[lax.rem(y + d, group)]
    zs = lax.broadcasted_iota(jnp.int32, (n_z, 1, 1), 0)
    pre = jnp.where(zs == z, rhs_ref[...][None], 0.0) - pre
    hi, lo = split(pre.reshape(sub, width))
    pre_s[0:sub, :] = hi
    pre_s[sub:, :] = lo
    for n in range(steps):
        at = slice(n * wide, (n + 1) * wide)
        below = slice(n * wide, width)
        both = mm(pre_s[:, below], diag_h[below, at])
        term = both[0:sub] + both[sub:] + mm(pre_s[0:sub, below], diag_l[below, at])
        acc[:, :, at] = term.reshape(n_z, share, wide)

    for k in range(1, n_col):
        pltpu.make_async_copy(low_ref.at[k], low_all.at[k, y], sem_low.at[k]).wait()

    def fold(i, carry):
        k = n_col - 1 - i
        for d in range(1, group):
            low_copy(k, lax.rem(y + d, group), y).wait_recv()
        h, l = split(low_all[k].reshape(depth, width))
        low_s[0:depth, :] = h
        low_s[depth:, :] = l
        for n in range(steps):
            at = slice(n * wide, (n + 1) * wide)
            below = slice(n * wide, width)
            both = mm(low_s[:, below], diag_h[below, at])
            term = both[0:depth] + both[depth:] + mm(low_s[0:depth, below], diag_l[below, at])
            h, l = split(term)
            fold_h[k, :, at] = h
            fold_l[k, :, at] = l
        return carry

    lax.fori_loop(0, n_col - 1 - col, fold, 0)

    def x_copy(k, owner, to, to_col):
        return pltpu.make_async_remote_copy(
            src_ref=solved.at[:, pl.ds(pl.multiple_of(to * depth, depth), depth)],
            dst_ref=x_in.at[k, owner],
            send_sem=x_tx.at[to_col, to],
            recv_sem=x_rx.at[k, owner],
            device_id=(to * group + y, to_col),
            device_id_type=MESH,
        )

    def absorb(i, carry):
        k = n_col - 1 - i
        for d in range(n_z):
            x_copy(k, d, z, col).wait_recv()
        h, l = split(x_in[k].reshape(sub, depth))
        x_s[0:sub, :] = h
        x_s[sub:, :] = l
        for n in range(steps):
            at = slice(n * wide, (n + 1) * wide)
            both = mm(x_s[...], fold_h[k, :, at])
            term = both[0:sub] + both[sub:] + mm(x_s[0:sub, :], fold_l[k, :, at])
            acc[:, :, at] = acc[:, :, at] - term.reshape(n_z, share, wide)
        return carry

    lax.fori_loop(0, n_col - 1 - col, absorb, 0)

    def red_copy(owner, to):
        return pltpu.make_async_remote_copy(
            src_ref=acc.at[to],
            dst_ref=red_in.at[owner],
            send_sem=red_tx.at[to],
            recv_sem=red_rx.at[owner],
            device_id=(to * group + y, col),
            device_id_type=MESH,
        )

    for d in range(1, n_z):
        red_copy(z, lax.rem(z + d, n_z)).start()
    total = acc[z]
    for d in range(1, n_z):
        at = lax.rem(z + d, n_z)
        red_copy(at, z).wait_recv()
        total = total + red_in[at]
    solved[...] = total

    def spread(i, carry):
        to_col = col - 1 - i
        for d in range(n_z):
            x_copy(col, z, lax.rem(z + d, n_z), to_col).start()
        return carry

    lax.fori_loop(0, col, spread, 0)
    out_ref[...] = total

    def spread_done(i, carry):
        to_col = col - 1 - i
        for d in range(n_z):
            x_copy(col, z, lax.rem(z + d, n_z), to_col).wait_send()
        return carry

    lax.fori_loop(0, col, spread_done, 0)
    for d in range(1, n_z):
        red_copy(z, lax.rem(z + d, n_z)).wait_send()
    for d in range(1, group):
        part_copy(y, lax.rem(y + d, group)).wait_send()
    for e in range(1, n_col):
        sel_copy(col, others_col(e)).wait_send()
    for k in range(n_col - 1, 0, -1):

        @pl.when(col < k)
        def _():
            for d in range(1, group):
                low_copy(k, y, lax.rem(y + d, group)).wait_send()


def on_device(
    n_row, n_col, anc_factor, anc_solution, slot_row, tile_count, lower_factor, diag_inverse, rhs
):
    panels, rows_local, width = lower_factor.shape
    slots = slot_row.shape[0]
    share = rhs.shape[0]
    n_rhs = share * n_row
    group = max(2, LANES // rows_local)
    n_z = n_row // group
    depth = group * rows_local
    sub = share * n_z
    mine, parents = anc_solution.shape
    dma = pltpu.SemaphoreType.DMA
    vmem = pltpu.VMEM
    in_vmem = pl.BlockSpec(memory_space=pltpu.VMEM)
    anywhere = pl.BlockSpec(memory_space=pl.ANY)
    return pl.pallas_call(
        functools.partial(kernel, group, n_row, n_col),
        out_shape=jax.ShapeDtypeStruct(rhs.shape, F32),
        in_specs=[
            in_vmem,
            pl.BlockSpec(memory_space=pltpu.SMEM),
            in_vmem,
            in_vmem,
            anywhere,
            anywhere,
            anywhere,
        ],
        out_specs=in_vmem,
        scratch_shapes=[
            vmem((slots, width), F32),
            vmem((slots, width), BF16),
            vmem((slots, width), BF16),
            vmem((width, width), F32),
            vmem((width, width), BF16),
            vmem((width, width), BF16),
            vmem((panels, group, rows_local, width), F32),
            vmem((2 * depth, width), BF16),
            vmem((panels, depth, width), BF16),
            vmem((panels, depth, width), BF16),
            vmem((2 * mine, parents), BF16),
            vmem((n_col, mine, slots), F32),
            vmem((2 * n_rhs, slots), BF16),
            vmem((group, n_z, share, width), F32),
            vmem((group, n_z, share, width), F32),
            vmem((2 * sub, width), BF16),
            vmem((n_z, share, width), F32),
            vmem((n_z, share, width), F32),
            vmem((share, width), F32),
            vmem((panels, n_z, share, depth), F32),
            vmem((2 * sub, depth), BF16),
            dma,
            dma,
            dma((panels,)),
            dma((n_col,)),
            dma((n_col,)),
            dma((panels, group)),
            dma((panels, group)),
            dma((group,)),
            dma((group,)),
            dma((n_z,)),
            dma((n_z,)),
            dma((n_col, n_z)),
            dma((panels, n_z)),
        ],
        compiler_params=pltpu.CompilerParams(
            collective_id=0, has_side_effects=True, vmem_limit_bytes=52 * 1024 * 1024
        ),
        name="front_solve",
    )(slot_row[None, :], tile_count, anc_solution, rhs, anc_factor, lower_factor, diag_inverse)


def solution(mesh):
    in_specs = (
        P("row", "col"),
        P("col", "row"),
        P("row"),
        P("row"),
        P(None, "row", "col"),
        P("col", None, None),
        P("row", "col"),
    )
    body = functools.partial(on_device, mesh.shape["row"], mesh.shape["col"])
    return jax.shard_map(
        body, mesh=mesh, in_specs=in_specs, out_specs=P("row", "col"), check_vma=False
    )
```
